32 devices in a mesh: dp: 2 (over core), expert: 16 (over z, y, x).
Axes of the slice: x: 2, y: 2, z: 4, core: 2. Of those that a mesh axis runs over, the one named last changes fastest.
Arguments:
- tokens: bfloat16 [2048, 2560], P(('dp', 'expert')), may hold values from -6 to 6
- cotangent: bfloat16 [2048, 2560], P(('dp', 'expert')), may hold values from -0.59765625 to 0.59765625
- w_gate: bfloat16 [16, 2560, 768], P('expert', 'dp'), may hold values from -0.125 to 0.125
- w_up: bfloat16 [16, 2560, 768], P('expert', 'dp'), may hold values from -0.125 to 0.125
- expert_ids: int32 [2048, 6], P(('dp', 'expert')), may hold values from 0 to 15, all different within a row; in each aligned block of 64 rows (0 to 63, 64 to 127, ...) at most 30 rows name the same one
- gate_num: int32 [2048, 6], P(('dp', 'expert')), may hold values from 1 to 64
- swap_flags: int32 [8], replicated, may hold values 0 or 1
Outputs:
- grad_held: float32 [16, 768, 2560], P('expert', 'dp')
The draws below stay inside these ranges and needn't reach their ends.
Inputs may be any that keep to these rules, and one draw needn't show every extreme that they name: `expert_ids`: each row names 6 different experts; the 64 rows of one device name no expert more than 30 times, a bound that some block reaches.
All inputs are finite; a program needn't handle non-finite values.
Results may differ from the reference program's by a relative error of at most 0.015.
Values may be sent and summed in bfloat16 or wider, within the bound.
A program may use at most 64 MiB of HBM per device.

```python
import math
import jax
import jax.numpy as jnp
import numpy as np
from jax import lax

D = 2560
FF = 768
TOPK = 6
TOK_DEV = 64
EXPERTS = 16
CAP = 30
TOKENS = 2048
N_DP = 2
N_EXPERT = 16


def plant(array, rng, least, high):
    longest = array.shape.index(max(array.shape))
    spots = []
    for shift in (0, 1):
        where = [jax.random.randint(jax.random.fold_in(rng, axis), (), 0, length) for axis, length in enumerate(array.shape)]
        where[longest] = (where[longest] + shift) % array.shape[longest]
        spots.append(tuple(where))
    return array.at[spots[0]].set(least).at[spots[1]].set(high)


def level_of(stream_key, dims, cuts, low, top_value):
    def one(dim, shards_of):
        draws = jax.random.uniform(jax.random.fold_in(jax.random.fold_in(stream_key, 6), dim), (shards_of,), jnp.float32, low / len(cuts), top_value / len(cuts))
        return jnp.repeat(jnp.exp(draws), dims[dim] // shards_of).reshape((-1,) + (1,) * (len(dims) - dim - 1))

    factor_of = one(*cuts[0])
    for cut in cuts[1:]:
        factor_of = factor_of * one(*cut)
    return factor_of


def assign_block(key, own, number, rows, number_of, top, most, skew):
    order = jax.random.permutation(key, number_of)
    crowded, ordinary = load_shares(number_of, rows * top, most, skew, True), load_shares(number_of, rows * top, most, skew, False)
    places = jnp.arange(number_of)

    def named(lengths, rotation):
        used = int((lengths > 0).sum())
        fixed = max(1, used // 4)
        shifted = fixed + (places - fixed + rotation * (used - fixed)) % max(1, number_of - fixed)
        return jnp.zeros((number_of,), jnp.int32).at[order[jnp.where(places < fixed, places, shifted)]].set(jnp.asarray(lengths, jnp.int32))

    lengths = jnp.where(number % 4 == 0, named(crowded, number // 4), named(ordinary, number - number // 4 - 1))
    mixed = jax.random.permutation(jax.random.fold_in(own, 3), number_of)
    donor, sink = mixed[0:number_of // 2 * 2:2], mixed[1:number_of // 2 * 2:2]
    room = jnp.minimum(lengths[donor] - 1, most - lengths[sink]) // 2
    room = jnp.where((donor == order[0]) | (sink == order[0]) | (lengths[sink] == 0), 0, jnp.maximum(room, 0))
    shifted = jax.random.randint(jax.random.fold_in(own, 4), (number_of // 2,), 0, 1 << 20) % (room + 1)
    lengths = lengths.at[donor].add(-shifted).at[sink].add(shifted)
    items = jnp.searchsorted(jnp.cumsum(lengths), jnp.arange(rows * top), side="right").astype(jnp.int32)
    grid = items.reshape(top, rows).T
    grid = grid[jax.random.permutation(jax.random.fold_in(own, 1), rows)]
    rotation = jax.random.randint(jax.random.fold_in(own, 2), (rows, 1), 0, top)
    return jnp.take_along_axis(grid, (jnp.arange(top)[None, :] + rotation) % top, axis=1)


def load_shares(number_of, total, most, lean, full):
    portions = [(1 << 20) // math.isqrt(standing ** lean) + 1 for standing in range(1, number_of + 1)]
    largest = most if full else min(most, max(-(-total // number_of), total * portions[0] // sum(portions)))
    least = 1 if total - largest >= number_of - 1 else 0
    counts, surplus = [largest] + [least] * (number_of - 1), total - largest - least * (number_of - 1)
    while surplus > 0:
        movable = [i for i in range(1, number_of) if counts[i] < largest] or [i for i in range(1, number_of) if counts[i] < most]
        pool, budget = sum([portions[i] for i in movable]), surplus
        for i in movable:
            addition = min(most - counts[i], max(1, budget * portions[i] // pool), surplus)
            counts[i] = counts[i] + addition
            surplus = surplus - addition
    return np.array(counts)


def normal_values(rng, extent, deviation, bound, pieces=(), kind=jnp.bfloat16):
    loudness = level_of(rng, extent, pieces, -0.22, 0.18) if pieces else 1.0
    array = jax.random.normal(rng, extent, jnp.float32) * deviation * loudness
    return jnp.minimum(jnp.maximum(array, -bound), bound).astype(kind)


def setup_inputs(seed: int = 0) -> dict:
    key_of = jax.random.split(jax.random.key(seed), 8)
    tokens = normal_values(key_of[0], (TOKENS, D), 1.0, 6.0, ((0, 32),))
    cotangent = normal_values(key_of[1], (TOKENS, D), 0.1, 0.59765625, ((0, 32),))
    w_gate = normal_values(key_of[2], (EXPERTS, D, FF), D ** -0.5, 0.125, ((0, 16), (1, 2)))
    w_up = normal_values(key_of[3], (EXPERTS, D, FF), D ** -0.5, 0.125, ((0, 16), (1, 2)))
    expert_ids_keys = jax.random.split(jax.random.fold_in(key_of[4], 1), TOKENS // TOK_DEV)
    expert_ids_turns = jax.random.permutation(jax.random.fold_in(key_of[4], 3), TOKENS // TOK_DEV)
    expert_ids = jax.vmap(lambda own, number: assign_block(jax.random.fold_in(key_of[4], 2), own, number, TOK_DEV, EXPERTS, TOPK, CAP, 2))(expert_ids_keys, expert_ids_turns).reshape((TOKENS, TOPK))
    gate_num = plant(jax.random.randint(key_of[5], (TOKENS, TOPK), 1, 65), jax.random.fold_in(key_of[5], 1), 1, 64).astype(jnp.int32)
    swap_flags = plant((jax.random.randint(key_of[6], (EXPERTS // 2,), 0, 2) < 1).astype(jnp.int32), jax.random.fold_in(key_of[6], 1), 0, 1)
    return dict(tokens=tokens, cotangent=cotangent, w_gate=w_gate, w_up=w_up, expert_ids=expert_ids, gate_num=gate_num, swap_flags=swap_flags)


def expert_terms(x_rows, dy_rows, ids_rows, num_rows, w_gate, w_up):
    assigned = ids_rows.reshape(-1).astype(jnp.int32)
    total = assigned.shape[0]
    one_hot = (assigned[:, None] == jnp.arange(EXPERTS, dtype=jnp.int32)[None, :]).astype(jnp.int32)
    ranking = jnp.sum((jnp.cumsum(one_hot, axis=0) - one_hot) * one_hot, axis=1).astype(jnp.int32)
    slot_count = N_EXPERT * CAP
    table = jnp.full((EXPERTS, slot_count), total, jnp.int32)
    table = table.at[assigned, ranking].set(jnp.arange(total, dtype=jnp.int32))
    usable = table < total
    clipped = jnp.minimum(table, total - 1).astype(jnp.int32)
    token_index = (clipped // TOPK).astype(jnp.int32)
    numbers = num_rows.reshape(-1)[clipped].astype(jnp.float32)
    weights = jnp.where(usable, numbers / 64.0, jnp.float32(0.0)).astype(jnp.float32)

    def one_expert(inputs):
        index_row, weight_row, gate_matrix, up_matrix = inputs
        chosen = x_rows[index_row]
        gate = jnp.dot(chosen, gate_matrix, preferred_element_type=jnp.float32)
        upper = jnp.dot(chosen, up_matrix, preferred_element_type=jnp.float32)
        hidden = (jax.nn.silu(gate) * upper).astype(jnp.bfloat16)
        scaled = (weight_row[:, None] * dy_rows[index_row].astype(jnp.float32)).astype(jnp.bfloat16)
        term = lax.dot_general(hidden, scaled, (((0,), (0,)), ((), ())), preferred_element_type=jnp.float32)
        term = lax.optimization_barrier(term.astype(jnp.bfloat16))
        return term.astype(jnp.float32)

    return lax.map(one_expert, (token_index, weights, w_gate, w_up))


def reference(tokens, cotangent, w_gate, w_up, expert_ids, gate_num, swap_flags):
    group_rows = TOK_DEV * N_EXPERT

    def add_group(index, accumulated):
        start = (index * group_rows).astype(jnp.int32)
        x_rows = lax.dynamic_slice_in_dim(tokens, start, group_rows, 0)
        dy_rows = lax.dynamic_slice_in_dim(cotangent, start, group_rows, 0)
        ids_rows = lax.dynamic_slice_in_dim(expert_ids, start, group_rows, 0)
        num_rows = lax.dynamic_slice_in_dim(gate_num, start, group_rows, 0)
        return accumulated + expert_terms(x_rows, dy_rows, ids_rows, num_rows, w_gate, w_up)

    accumulated = lax.fori_loop(0, N_DP, add_group, jnp.zeros((EXPERTS, FF, D), jnp.float32))
    half_count = EXPERTS // 2
    experts = jnp.arange(EXPERTS, dtype=jnp.int32)
    held = jnp.where(swap_flags[experts % half_count] == 1, (experts + half_count) % EXPERTS, experts).astype(jnp.int32)
    return accumulated[held]
```

```python
import jax
import jax.numpy as jnp
from jax import lax
from jax.sharding import PartitionSpec as P


def from_partner(value, axis, apart):
    return lax.ppermute(value, axis, [(i, i ^ 1 << apart) for i in range(lax.axis_size(axis))])


def shards(tokens, cotangent, w_gate, w_up, expert_ids, gate_num, swap_flags):
    expert_count = lax.axis_size("expert")
    half_count = expert_count // 2
    swap_bit = expert_count.bit_length() - 2
    my_index = lax.axis_index("expert")
    tok_count, top_count = expert_ids.shape
    capacity = 5 * tok_count * top_count // (4 * expert_count)
    width = tokens.shape[1]
    my_flag = swap_flags[my_index % half_count] == 1
    flat_ids = expert_ids.reshape(-1)
    columns = jnp.arange(expert_count, dtype=jnp.int32)
    one_hot = (flat_ids[:, None] == columns[None, :]).astype(jnp.int32)
    ranking = jnp.sum((jnp.cumsum(one_hot, axis=0) - one_hot) * one_hot, axis=1)
    slot_ids = jnp.arange(expert_count * capacity, dtype=jnp.int32)

    def picked_by(destination):
        slot = destination * capacity + ranking
        return (slot_ids[:, None] == slot[None, :]).reshape(
            expert_count * capacity, tok_count, top_count
        )

    token_map = jnp.sum(picked_by(flat_ids).astype(jnp.int32), axis=2).astype(jnp.bfloat16)
    holder = jnp.where(
        swap_flags[flat_ids % half_count] == 1, (flat_ids + half_count) % expert_count, flat_ids
    )
    fractions = gate_num.astype(jnp.float32) / 64.0
    weight_map = jnp.sum(jnp.where(picked_by(holder), fractions[None], 0.0), axis=2).astype(jnp.bfloat16)
    send_rows = jnp.dot(token_map, tokens, preferred_element_type=jnp.float32).astype(jnp.bfloat16)
    send_grads = jnp.dot(weight_map, cotangent, preferred_element_type=jnp.float32).astype(
        jnp.bfloat16
    )

    def exchange(value):
        value = value.reshape(expert_count, capacity, width)
        value = lax.all_to_all(value, "expert", split_axis=0, concat_axis=0, tiled=True)
        return value.reshape(expert_count * capacity, width)

    gate_rows = lax.all_gather(w_gate[0], "dp", axis=0, tiled=True)
    up_rows = lax.all_gather(w_up[0], "dp", axis=0, tiled=True)
    recv_rows = exchange(send_rows)
    gate_sum = jnp.dot(recv_rows, gate_rows, preferred_element_type=jnp.float32)
    up_sum = jnp.dot(recv_rows, up_rows, preferred_element_type=jnp.float32)
    hidden = (jax.nn.silu(gate_sum) * up_sum).astype(jnp.bfloat16)
    other = from_partner(hidden, "expert", swap_bit)
    recv_grads = exchange(send_grads)
    hidden = jnp.where(my_flag, other, hidden)
    grads = lax.psum_scatter(
        lax.dot_general(
            hidden, recv_grads, (((0,), (0,)), ((), ())), preferred_element_type=jnp.float32
        ).astype(jnp.bfloat16),
        "dp",
        scatter_dimension=0,
        tiled=True,
    ).astype(jnp.float32)
    return grads[None]


def solution(mesh):
    in_specs = (
        P(("dp", "expert"), None),
        P(("dp", "expert"), None),
        P("expert", "dp", None),
        P("expert", "dp", None),
        P(("dp", "expert"), None),
        P(("dp", "expert"), None),
        P(),
    )
    out_specs = P("expert", "dp", None)
    return jax.shard_map(shards, mesh=mesh, in_specs=in_specs, out_specs=out_specs, check_vma=False)
```

```python
import jax
import jax.numpy as jnp
from jax import lax
from jax.experimental import pallas as pl
from jax.experimental.pallas import tpu as pltpu
from jax.sharding import PartitionSpec as P


def from_partner(value, axis, apart):
    return lax.ppermute(value, axis, [(i, i ^ 1 << apart) for i in range(lax.axis_size(axis))])


def shards(tokens, cotangent, w_gate, w_up, expert_ids, gate_num, swap_flags):
    expert_count = lax.axis_size("expert")
    half_count = expert_count // 2
    swap_bit = expert_count.bit_length() - 2
    my_index = lax.axis_index("expert")
    tok_count, top_count = expert_ids.shape
    capacity = 5 * tok_count * top_count // (4 * expert_count)
    width = tokens.shape[1]
    my_flag = swap_flags[my_index % half_count] == 1
    flat_ids = expert_ids.reshape(-1)
    columns = jnp.arange(expert_count, dtype=jnp.int32)
    one_hot = (flat_ids[:, None] == columns[None, :]).astype(jnp.int32)
    ranking = jnp.sum((jnp.cumsum(one_hot, axis=0) - one_hot) * one_hot, axis=1)
    slot_ids = jnp.arange(expert_count * capacity, dtype=jnp.int32)

    def picked_by(destination):
        slot = destination * capacity + ranking
        return (slot_ids[:, None] == slot[None, :]).reshape(
            expert_count * capacity, tok_count, top_count
        )

    token_map = jnp.sum(picked_by(flat_ids).astype(jnp.int32), axis=2).astype(jnp.bfloat16)
    holder = jnp.where(
        swap_flags[flat_ids % half_count] == 1, (flat_ids + half_count) % expert_count, flat_ids
    )
    fractions = gate_num.astype(jnp.float32) / 64.0
    weight_map = jnp.sum(jnp.where(picked_by(holder), fractions[None], 0.0), axis=2).astype(jnp.bfloat16)
    send_rows = jnp.dot(token_map, tokens, preferred_element_type=jnp.float32).astype(jnp.bfloat16)
    send_grads = jnp.dot(weight_map, cotangent, preferred_element_type=jnp.float32).astype(
        jnp.bfloat16
    )

    def exchange(value):
        value = value.reshape(expert_count, capacity, width)
        value = lax.all_to_all(value, "expert", split_axis=0, concat_axis=0, tiled=True)
        return value.reshape(expert_count * capacity, width)

    gate_rows = lax.all_gather(w_gate[0], "dp", axis=0, tiled=True)
    up_rows = lax.all_gather(w_up[0], "dp", axis=0, tiled=True)
    recv_rows = exchange(send_rows)
    gate_sum = jnp.dot(recv_rows, gate_rows, preferred_element_type=jnp.float32)
    up_sum = jnp.dot(recv_rows, up_rows, preferred_element_type=jnp.float32)
    hidden = (jax.nn.silu(gate_sum) * up_sum).astype(jnp.bfloat16)
    other = from_partner(hidden, "expert", swap_bit)
    recv_grads = exchange(send_grads)
    hidden = jnp.where(my_flag, other, hidden)
    grads = lax.psum_scatter(
        lax.dot_general(
            hidden, recv_grads, (((0,), (0,)), ((), ())), preferred_element_type=jnp.float32
        ).astype(jnp.bfloat16),
        "dp",
        scatter_dimension=0,
        tiled=True,
    ).astype(jnp.float32)
    return grads[None]


ZS, LANES, SLOTS, TILES = 4, 128, 32, 5


def kernel(flags_ref, ids_ref, num_ref, tok_hbm, cot_hbm, wg_hbm, wu_hbm, out_ref,
           tok, cot, wg, wu, picked, hid, hid_other, hid_t, scaled, part, part_other,
           local_sem, z_send, z_recv, c_send, c_recv, d_send, d_recv,
           w_send, w_recv, h_send, h_recv, p_send, p_recv):
    rows, width = tok_hbm.shape
    count = ids_ref.shape[1]
    half, ff = wg_hbm.shape
    mine = ff // 2
    experts = 4 * ZS
    dp, me = lax.axis_index("dp"), lax.axis_index("expert")
    x, y, z = me % 2, (me // 2) % 2, me // 4
    to_x, to_y = (dp, me + 1 - 2 * x), (dp, me + 2 - 4 * y)
    up, down = (dp, me + 4), (dp, me - 4)
    pair = (dp, (me + 8) % experts)
    twin = (1 - dp, me)
    col, x_col, y_col = me % 4, me % 4 + 1 - 2 * x, me % 4 + 2 - 4 * y
    d_col = 3 - col

    barrier = pltpu.get_barrier_semaphore()

    def greet(device):
        pl.semaphore_signal(barrier, inc=1, device_id=device, device_id_type=pl.DeviceIdType.MESH)

    for device in (to_x, to_y, pair, twin):
        greet(device)
    pl.when(z < ZS - 1)(lambda: greet(up))
    pl.when(z > 0)(lambda: greet(down))

    def shard(column, s):
        return pl.ds(pl.multiple_of((column * ZS + z + s) * rows, rows), rows)

    def remote(ref, send, recv, device, target=None):
        return pltpu.make_async_remote_copy(
            src_ref=ref, dst_ref=ref if target is None else target, send_sem=send, recv_sem=recv,
            device_id=device, device_id_type=pl.DeviceIdType.MESH)

    own = shard(col, 0)
    loads = [
        pltpu.make_async_copy(tok_hbm, tok.at[own, pl.ds(0, width)], local_sem.at[0]),
        pltpu.make_async_copy(cot_hbm, cot.at[own], local_sem.at[1]),
        pltpu.make_async_copy(wg_hbm, wg.at[dp], local_sem.at[2]),
        pltpu.make_async_copy(wu_hbm, wu.at[dp], local_sem.at[3]),
    ]
    for load in loads:
        load.start()

    lanes = lax.broadcasted_iota(jnp.int32, (rows, LANES), 1)
    fractions = num_ref[...].astype(jnp.float32) / 64.0
    table = jnp.zeros((rows, LANES), jnp.float32)
    for k in range(count):
        table = jnp.where(lanes == ids_ref[:, k:k + 1], fractions[:, k:k + 1], table)
    tok[own, pl.ds(width, LANES)] = table.astype(jnp.bfloat16)

    inner = (z > 0) & (z < ZS - 1)
    pl.when(inner)(lambda: pl.semaphore_wait(barrier, 6))
    pl.when(jnp.logical_not(inner))(lambda: pl.semaphore_wait(barrier, 5))

    arrays = (tok, cot)

    def valid(s):
        return z + s >= 0 if s < 0 else z + s < ZS

    def z_copy(a, way, d, s):
        return remote(arrays[a].at[shard(col, s)], z_send.at[a, way, d], z_recv.at[a, way, d],
                      up if way == 0 else down)

    def c_copy(a, way, s, column):
        return remote(arrays[a].at[shard(column, s)], c_send.at[a, way, s + 3],
                      c_recv.at[a, way, s + 3], to_x if way == 0 else to_y)

    def d_copy(a, way, s, column):
        start = (column * ZS + z + s) * rows + way * (rows // 2)
        return remote(arrays[a].at[pl.ds(pl.multiple_of(start, rows // 2), rows // 2)],
                      d_send.at[a, way, s + 3], d_recv.at[a, way, s + 3], to_x if way == 0 else to_y)

    def z_sends(a, s, act):
        if -3 < s <= 0:
            pl.when(z < ZS - 1)(lambda: act(z_copy(a, 0, -s, s)))
        if 0 <= s < 3:
            pl.when(z > 0)(lambda: act(z_copy(a, 1, s, s)))

    def begin(copy):
        copy.start()

    def own_plane(a, s):
        c_copy(a, 0, s, col).start()
        c_copy(a, 1, s, col).start()

    def step_z(a, d):
        for s in (-d, d):
            @pl.when(valid(s))
            def _(s=s):
                z_copy(a, 0 if s < 0 else 1, d - 1, s).wait_recv()
                z_sends(a, s, begin)
                own_plane(a, s)

    def step_plane(a, d):
        for s in ((0,) if d == 0 else (-d, d)):
            @pl.when(valid(s))
            def _(s=s):
                c_copy(a, 1, s, y_col).wait_recv()
                d_copy(a, 0, s, y_col).start()
                c_copy(a, 0, s, x_col).wait_recv()
                d_copy(a, 1, s, x_col).start()

    def step_diagonal(a):
        for s in range(-3, 4):
            @pl.when(valid(s))
            def _(s=s):
                d_copy(a, 0, s, d_col).wait_recv()
                d_copy(a, 1, s, d_col).wait_recv()

    chunk = ZS * rows
    packed = ZS * SLOTS
    flag = flags_ref[me % (experts // 2)]
    held = jnp.where(flag == 1, (me + experts // 2) % experts, me)
    t0 = lax.broadcasted_iota(jnp.int32, (chunk, chunk), 0)
    t1 = lax.broadcasted_iota(jnp.int32, (chunk, chunk), 1)
    earlier = jnp.where((t0 < t1) & (t0 // rows == t1 // rows), 1.0, 0.0).astype(jnp.bfloat16)

    def chosen(column, expert, weighted):
        r = pl.ds(pl.multiple_of(column * chunk, chunk), chunk)
        one = jnp.where(lax.broadcasted_iota(jnp.int32, (16, LANES), 1) == expert, 1.0, 0.0)
        weight = lax.dot_general(one.astype(jnp.bfloat16), tok[r, pl.ds(width, LANES)],
                                 (((1,), (1,)), ((), ())), preferred_element_type=jnp.float32)
        named = jnp.where(weight > 0.0, 1.0, 0.0)
        rank = jnp.dot(named.astype(jnp.bfloat16), earlier, preferred_element_type=jnp.float32)
        place = lax.broadcasted_iota(jnp.int32, (packed, chunk), 0)
        token = lax.broadcasted_iota(jnp.int32, (packed, chunk), 1)
        goal = (place % SLOTS).astype(jnp.float32)
        hit = (goal == rank[0:1]) & (place // SLOTS == token // rows) & (weight[0:1] > 0.0)
        value = weight[0:1] if weighted else named[0:1]
        return jnp.where(hit, value, 0.0).astype(jnp.bfloat16)

    def h_copy(k, column):
        r = pl.ds(pl.multiple_of(column * packed, packed), packed)
        return remote(hid.at[r], h_send.at[k], h_recv.at[k], pair, hid_other.at[r])

    def hidden(k, column):
        r = pl.ds(pl.multiple_of(column * chunk, chunk), chunk)
        h = pl.ds(pl.multiple_of(column * packed, packed), packed)
        take = chosen(column, me, False)

        @pl.loop(0, width // 512)
        def _(n):
            c = pl.ds(pl.multiple_of(n * 512, 512), 512)
            picked[:, c] = jnp.dot(take, tok[r, c], preferred_element_type=jnp.float32).astype(jnp.bfloat16)

        @pl.loop(0, ff // 256)
        def _(n):
            c = pl.ds(pl.multiple_of(n * 256, 256), 256)
            lo, hi = picked[:, 0:half], picked[:, half:2 * half]

            def project(w):
                return (jnp.dot(lo, w[0, :, c], preferred_element_type=jnp.float32)
                        + jnp.dot(hi, w[1, :, c], preferred_element_type=jnp.float32))

            gate, upper = project(wg), project(wu)
            hid[h, c] = (gate / (1.0 + jnp.exp(-gate)) * upper).astype(jnp.bfloat16)

        h_copy(k, column).start()

    def scale(column):
        r = pl.ds(pl.multiple_of(column * chunk, chunk), chunk)
        h = pl.ds(pl.multiple_of(column * packed, packed), packed)
        take = chosen(column, held, True)

        @pl.loop(0, width // 512)
        def _(n):
            c = pl.ds(pl.multiple_of(n * 512, 512), 512)
            scaled[h, c] = jnp.dot(take, cot[r, c], preferred_element_type=jnp.float32).astype(jnp.bfloat16)

    loads[0].wait()
    z_sends(0, 0, begin)
    own_plane(0, 0)
    weights = [remote(wg_hbm, w_send.at[0], w_recv.at[0], twin, wg.at[dp]),
               remote(wu_hbm, w_send.at[1], w_recv.at[1], twin, wu.at[dp])]
    for copy in weights:
        copy.start()
    loads[1].wait()
    step_z(0, 1)
    step_plane(0, 0)
    step_z(0, 2)
    z_sends(1, 0, begin)
    step_plane(0, 1)
    step_z(0, 3)
    loads[2].wait()
    loads[3].wait()
    remote(wg.at[1 - dp], w_send.at[0], w_recv.at[0], twin).wait_recv()
    remote(wu.at[1 - dp], w_send.at[1], w_recv.at[1], twin).wait_recv()
    hidden(0, col)
    step_plane(0, 2)
    step_plane(0, 3)
    own_plane(1, 0)
    step_z(1, 1)
    hidden(1, y_col)
    hidden(2, x_col)
    step_z(1, 2)
    step_z(1, 3)
    step_diagonal(0)
    hidden(3, d_col)
    for d in range(4):
        step_plane(1, d)
    for column in (col, y_col, x_col):
        scale(column)
    for k, column in enumerate((col, y_col, x_col, d_col)):
        h_copy(k, column).wait_recv()
    hid_t[...] = jnp.where(flag == 1, hid_other[...].astype(jnp.float32),
                           hid[...].astype(jnp.float32)).T.astype(jnp.bfloat16)
    step_diagonal(1)
    scale(d_col)

    tile = width // TILES

    def product(core, n):
        r = pl.ds(pl.multiple_of(core * mine, mine), mine)
        c = pl.ds(pl.multiple_of(n * tile, tile), tile)
        return jnp.dot(hid_t[r], scaled[:, c], preferred_element_type=jnp.float32).astype(jnp.bfloat16)

    def p_copy(n):
        return remote(part.at[n], p_send.at[n], p_recv.at[n], twin, part_other.at[n])

    for n in range(TILES):
        part[n] = product(1 - dp, n)
        p_copy(n).start()
    for n in range(TILES):
        out_ref[:, n * tile:(n + 1) * tile] = product(dp, n).astype(jnp.float32)
    for n in range(TILES):
        p_copy(n).wait_recv()
        out_ref[:, n * tile:(n + 1) * tile] += part_other[n].astype(jnp.float32)

    for a in range(2):
        for s in range(-3, 4):
            @pl.when(valid(s))
            def _(a=a, s=s):
                z_sends(a, s, lambda copy: copy.wait_send())
                for way in range(2):
                    c_copy(a, way, s, col).wait_send()
                d_copy(a, 0, s, y_col).wait_send()
                d_copy(a, 1, s, x_col).wait_send()
    for copy in weights:
        copy.wait_send()
    for k, column in enumerate((col, y_col, x_col, d_col)):
        h_copy(k, column).wait_send()
    for n in range(TILES):
        p_copy(n).wait_send()


def fused(tokens, cotangent, w_gate, w_up, expert_ids, gate_num, swap_flags):
    rows, width = tokens.shape
    _, half, ff = w_gate.shape
    total, packed = 16 * rows, 16 * SLOTS
    bf16, dma = jnp.bfloat16, pltpu.SemaphoreType.DMA
    hbm, vmem = pl.BlockSpec(memory_space=pl.ANY), pl.BlockSpec(memory_space=pltpu.VMEM)
    grads = pl.pallas_call(
        kernel,
        out_shape=jax.ShapeDtypeStruct((ff // 2, width), jnp.float32),
        in_specs=[pl.BlockSpec(memory_space=pltpu.SMEM), vmem, vmem, hbm, hbm, hbm, hbm],
        out_specs=vmem,
        scratch_shapes=[
            pltpu.VMEM((total, width + LANES), bf16),
            pltpu.VMEM((total, width), bf16),
            pltpu.VMEM((2, half, ff), bf16),
            pltpu.VMEM((2, half, ff), bf16),
            pltpu.VMEM((ZS * SLOTS, width), bf16),
            pltpu.VMEM((packed, ff), bf16),
            pltpu.VMEM((packed, ff), bf16),
            pltpu.VMEM((ff, packed), bf16),
            pltpu.VMEM((packed, width), bf16),
            pltpu.VMEM((TILES, ff // 2, width // TILES), bf16),
            pltpu.VMEM((TILES, ff // 2, width // TILES), bf16),
            dma((4,)), dma((2, 2, 3)), dma((2, 2, 3)), dma((2, 2, 7)), dma((2, 2, 7)),
            dma((2, 2, 7)), dma((2, 2, 7)), dma((2,)), dma((2,)), dma((4,)), dma((4,)),
            dma((TILES,)), dma((TILES,)),
        ],
        compiler_params=pltpu.CompilerParams(
            collective_id=0, has_side_effects=True, vmem_limit_bytes=52 * 1024 * 1024),
        cost_estimate=pl.CostEstimate(flops=8 * 10**9, bytes_accessed=2 * 10**7, transcendentals=400000),
    )(swap_flags, expert_ids, gate_num, tokens, cotangent, w_gate[0], w_up[0])
    return grads[None]


def solution(mesh):
    small = mesh.shape["expert"] == 16 and mesh.shape["dp"] == 2
    in_specs = (
        P(("dp", "expert"), None),
        P(("dp", "expert"), None),
        P("expert", "dp", None),
        P("expert", "dp", None),
        P(("dp", "expert"), None),
        P(("dp", "expert"), None),
        P(),
    )
    out_specs = P("expert", "dp", None)
    return jax.shard_map(fused if small else shards, mesh=mesh, in_specs=in_specs, out_specs=out_specs, check_vma=False)
```

```python
import jax
import jax.numpy as jnp
from jax import lax
from jax.experimental import pallas as pl
from jax.experimental.pallas import tpu as pltpu
from jax.sharding import PartitionSpec as P


def from_partner(value, axis, apart):
    return lax.ppermute(value, axis, [(i, i ^ 1 << apart) for i in range(lax.axis_size(axis))])


def shards(tokens, cotangent, w_gate, w_up, expert_ids, gate_num, swap_flags):
    expert_count = lax.axis_size("expert")
    half_count = expert_count // 2
    swap_bit = expert_count.bit_length() - 2
    my_index = lax.axis_index("expert")
    tok_count, top_count = expert_ids.shape
    capacity = 5 * tok_count * top_count // (4 * expert_count)
    width = tokens.shape[1]
    my_flag = swap_flags[my_index % half_count] == 1
    flat_ids = expert_ids.reshape(-1)
    columns = jnp.arange(expert_count, dtype=jnp.int32)
    one_hot = (flat_ids[:, None] == columns[None, :]).astype(jnp.int32)
    ranking = jnp.sum((jnp.cumsum(one_hot, axis=0) - one_hot) * one_hot, axis=1)
    slot_ids = jnp.arange(expert_count * capacity, dtype=jnp.int32)

    def picked_by(destination):
        slot = destination * capacity + ranking
        return (slot_ids[:, None] == slot[None, :]).reshape(
            expert_count * capacity, tok_count, top_count
        )

    token_map = jnp.sum(picked_by(flat_ids).astype(jnp.int32), axis=2).astype(jnp.bfloat16)
    holder = jnp.where(
        swap_flags[flat_ids % half_count] == 1, (flat_ids + half_count) % expert_count, flat_ids
    )
    fractions = gate_num.astype(jnp.float32) / 64.0
    weight_map = jnp.sum(jnp.where(picked_by(holder), fractions[None], 0.0), axis=2).astype(jnp.bfloat16)
    send_rows = jnp.dot(token_map, tokens, preferred_element_type=jnp.float32).astype(jnp.bfloat16)
    send_grads = jnp.dot(weight_map, cotangent, preferred_element_type=jnp.float32).astype(
        jnp.bfloat16
    )

    def exchange(value):
        value = value.reshape(expert_count, capacity, width)
        value = lax.all_to_all(value, "expert", split_axis=0, concat_axis=0, tiled=True)
        return value.reshape(expert_count * capacity, width)

    gate_rows = lax.all_gather(w_gate[0], "dp", axis=0, tiled=True)
    up_rows = lax.all_gather(w_up[0], "dp", axis=0, tiled=True)
    recv_rows = exchange(send_rows)
    gate_sum = jnp.dot(recv_rows, gate_rows, preferred_element_type=jnp.float32)
    up_sum = jnp.dot(recv_rows, up_rows, preferred_element_type=jnp.float32)
    hidden = (jax.nn.silu(gate_sum) * up_sum).astype(jnp.bfloat16)
    other = from_partner(hidden, "expert", swap_bit)
    recv_grads = exchange(send_grads)
    hidden = jnp.where(my_flag, other, hidden)
    grads = lax.psum_scatter(
        lax.dot_general(
            hidden, recv_grads, (((0,), (0,)), ((), ())), preferred_element_type=jnp.float32
        ).astype(jnp.bfloat16),
        "dp",
        scatter_dimension=0,
        tiled=True,
    ).astype(jnp.float32)
    return grads[None]


ZS, LANES, SLOTS, TILES = 4, 128, 32, 5


def kernel(flags_ref, ids_hbm, num_hbm, tok_hbm, cot_hbm, wg_hbm, wu_hbm, sum_hbm, other_hbm,
           tok, cot, wg, wu, picked, hid, hid_other, hid_t, scaled, part, part_own, ids_ref, num_ref,
           local_sem, z_send, z_recv, c_send, c_recv, d_send, d_recv, e_send, e_recv, o_sem,
           w_send, w_recv, h_send, h_recv, p_send, p_recv):
    rows, width = tok_hbm.shape
    count = ids_hbm.shape[0]
    half, ff = wg_hbm.shape
    mine = ff // 2
    experts = 4 * ZS
    dp, me = lax.axis_index("dp"), lax.axis_index("expert")
    x, y, z = me % 2, (me // 2) % 2, me // 4
    to_x, to_y = (dp, me + 1 - 2 * x), (dp, me + 2 - 4 * y)
    up, down = (dp, me + 4), (dp, me - 4)
    pair = (dp, (me + 8) % experts)
    twin = (1 - dp, me)
    col, x_col, y_col = me % 4, me % 4 + 1 - 2 * x, me % 4 + 2 - 4 * y
    d_col = 3 - col

    barrier = pltpu.get_barrier_semaphore()

    def greet(device):
        pl.semaphore_signal(barrier, inc=1, device_id=device, device_id_type=pl.DeviceIdType.MESH)

    for device in (to_x, to_y, pair, twin):
        greet(device)
    pl.when(z < ZS - 1)(lambda: greet(up))
    pl.when(z > 0)(lambda: greet(down))

    def shard(column, s):
        return pl.ds(pl.multiple_of((column * ZS + z + s) * rows, rows), rows)

    def remote(ref, send, recv, device, target=None):
        return pltpu.make_async_remote_copy(
            src_ref=ref, dst_ref=ref if target is None else target, send_sem=send, recv_sem=recv,
            device_id=device, device_id_type=pl.DeviceIdType.MESH)

    own = shard(col, 0)
    loads = [
        pltpu.make_async_copy(tok_hbm, tok.at[own, pl.ds(0, width)], local_sem.at[0]),
        pltpu.make_async_copy(cot_hbm, cot.at[own], local_sem.at[1]),
        pltpu.make_async_copy(wg_hbm, wg.at[dp], local_sem.at[2]),
        pltpu.make_async_copy(wu_hbm, wu.at[dp], local_sem.at[3]),
    ]
    names = [pltpu.make_async_copy(ids_hbm, ids_ref, local_sem.at[4]),
             pltpu.make_async_copy(num_hbm, num_ref, local_sem.at[5])]
    for load in names + loads:
        load.start()
    for load in names:
        load.wait()

    lanes = lax.broadcasted_iota(jnp.int32, (LANES, rows), 0)
    fractions = num_ref[...].astype(jnp.float32) / 64.0
    table = jnp.zeros((LANES, rows), jnp.float32)
    for k in range(count):
        table = jnp.where(lanes == ids_ref[k:k + 1, :], fractions[k:k + 1, :], table)
    same = (lax.broadcasted_iota(jnp.int32, (rows, rows), 0)
            == lax.broadcasted_iota(jnp.int32, (rows, rows), 1))
    tok[own, pl.ds(width, LANES)] = lax.dot_general(
        jnp.where(same, 1.0, 0.0).astype(jnp.bfloat16), table.astype(jnp.bfloat16),
        (((1,), (1,)), ((), ())), preferred_element_type=jnp.float32).astype(jnp.bfloat16)

    inner = (z > 0) & (z < ZS - 1)
    pl.when(inner)(lambda: pl.semaphore_wait(barrier, 6))
    pl.when(jnp.logical_not(inner))(lambda: pl.semaphore_wait(barrier, 5))

    arrays = (tok, cot)

    def valid(s):
        return z + s >= 0 if s < 0 else z + s < ZS

    def z_copy(a, way, d, s):
        return remote(arrays[a].at[shard(col, s)], z_send.at[a, way, d], z_recv.at[a, way, d],
                      up if way == 0 else down)

    def c_copy(a, way, s, column):
        return remote(arrays[a].at[shard(column, s)], c_send.at[a, way, s + 3],
                      c_recv.at[a, way, s + 3], to_x if way == 0 else to_y)

    def d_copy(a, way, s, column):
        size = rows // 2 if s == 0 else rows // 4
        start = (column * ZS + z + s) * rows + way * size
        return remote(arrays[a].at[pl.ds(pl.multiple_of(start, size), size)],
                      d_send.at[a, way, s + 3], d_recv.at[a, way, s + 3], to_x if way == 0 else to_y)

    def e_copy(a, way, d, s):
        start = (d_col * ZS + z + s) * rows + rows // 2
        return remote(arrays[a].at[pl.ds(pl.multiple_of(start, rows // 2), rows // 2)],
                      e_send.at[a, way, d], e_recv.at[a, way, d], up if way == 0 else down)

    def z_sends(a, s, act, copy=z_copy):
        if -3 < s <= 0:
            pl.when(z < ZS - 1)(lambda: act(copy(a, 0, -s, s)))
        if 0 <= s < 3:
            pl.when(z > 0)(lambda: act(copy(a, 1, s, s)))

    def begin(copy):
        copy.start()

    def own_plane(a, s):
        c_copy(a, 0, s, col).start()
        c_copy(a, 1, s, col).start()

    def step_z(a, d):
        for s in (-d, d):
            @pl.when(valid(s))
            def _(s=s):
                z_copy(a, 0 if s < 0 else 1, d - 1, s).wait_recv()
                z_sends(a, s, begin)
                own_plane(a, s)

    def step_plane(a, d):
        for s in ((0,) if d == 0 else (-d, d)):
            @pl.when(valid(s))
            def _(s=s):
                c_copy(a, 1, s, y_col).wait_recv()
                d_copy(a, 0, s, y_col).start()
                c_copy(a, 0, s, x_col).wait_recv()
                d_copy(a, 1, s, x_col).start()

    def step_e(a, d):
        if d == 0:
            d_copy(a, 1, 0, d_col).wait_recv()
            z_sends(a, 0, begin, e_copy)
            return
        for s in (-d, d):
            @pl.when(valid(s))
            def _(s=s):
                e_copy(a, 0 if s < 0 else 1, d - 1, s).wait_recv()
                z_sends(a, s, begin, e_copy)

    def step_diagonal(a):
        for s in range(-3, 4):
            @pl.when(valid(s))
            def _(s=s):
                d_copy(a, 0, s, d_col).wait_recv()
                if s != 0:
                    d_copy(a, 1, s, d_col).wait_recv()

    chunk = ZS * rows
    packed = ZS * SLOTS
    flag = flags_ref[me % (experts // 2)]
    held = jnp.where(flag == 1, (me + experts // 2) % experts, me)
    t0 = lax.broadcasted_iota(jnp.int32, (chunk, chunk), 0)
    t1 = lax.broadcasted_iota(jnp.int32, (chunk, chunk), 1)
    earlier = jnp.where((t0 < t1) & (t0 // rows == t1 // rows), 1.0, 0.0).astype(jnp.bfloat16)

    def chosen(column, expert, weighted):
        r = pl.ds(pl.multiple_of(column * chunk, chunk), chunk)
        one = jnp.where(lax.broadcasted_iota(jnp.int32, (16, LANES), 1) == expert, 1.0, 0.0)
        weight = lax.dot_general(one.astype(jnp.bfloat16), tok[r, pl.ds(width, LANES)],
                                 (((1,), (1,)), ((), ())), preferred_element_type=jnp.float32)
        named = jnp.where(weight > 0.0, 1.0, 0.0)
        rank = jnp.dot(named.astype(jnp.bfloat16), earlier, preferred_element_type=jnp.float32)
        place = lax.broadcasted_iota(jnp.int32, (packed, chunk), 0)
        token = lax.broadcasted_iota(jnp.int32, (packed, chunk), 1)
        goal = (place % SLOTS).astype(jnp.float32)
        hit = (goal == rank[0:1]) & (place // SLOTS == token // rows) & (weight[0:1] > 0.0)
        value = weight[0:1] if weighted else named[0:1]
        return jnp.where(hit, value, 0.0).astype(jnp.bfloat16)

    def h_copy(k, column):
        r = pl.ds(pl.multiple_of(column * packed, packed), packed)
        return remote(hid.at[r], h_send.at[k], h_recv.at[k], pair, hid_other.at[r])

    def hidden(k, column):
        r = pl.ds(pl.multiple_of(column * chunk, chunk), chunk)
        h = pl.ds(pl.multiple_of(column * packed, packed), packed)
        take = chosen(column, me, False)

        @pl.loop(0, width // 512)
        def _(n):
            c = pl.ds(pl.multiple_of(n * 512, 512), 512)
            picked[:, c] = jnp.dot(take, tok[r, c], preferred_element_type=jnp.float32).astype(jnp.bfloat16)

        @pl.loop(0, ff // 256)
        def _(n):
            c = pl.ds(pl.multiple_of(n * 256, 256), 256)
            lo, hi = picked[:, 0:half], picked[:, half:2 * half]

            def project(w):
                return (jnp.dot(lo, w[0, :, c], preferred_element_type=jnp.float32)
                        + jnp.dot(hi, w[1, :, c], preferred_element_type=jnp.float32))

            gate, upper = project(wg), project(wu)
            hid[h, c] = (gate / (1.0 + jnp.exp(-gate)) * upper).astype(jnp.bfloat16)

        h_copy(k, column).start()

    def scale(column):
        r = pl.ds(pl.multiple_of(column * chunk, chunk), chunk)
        h = pl.ds(pl.multiple_of(column * packed, packed), packed)
        take = chosen(column, held, True)

        @pl.loop(0, width // 512)
        def _(n):
            c = pl.ds(pl.multiple_of(n * 512, 512), 512)
            scaled[h, c] = jnp.dot(take, cot[r, c], preferred_element_type=jnp.float32).astype(jnp.bfloat16)

    loads[0].wait()
    z_sends(0, 0, begin)
    own_plane(0, 0)
    weights = [remote(wg_hbm, w_send.at[0], w_recv.at[0], twin, wg.at[dp]),
               remote(wu_hbm, w_send.at[1], w_recv.at[1], twin, wu.at[dp])]
    for copy in weights:
        copy.start()
    loads[1].wait()
    step_z(0, 1)
    step_plane(0, 0)
    step_z(0, 2)
    step_e(0, 0)
    z_sends(1, 0, begin)
    step_plane(0, 1)
    step_z(0, 3)
    step_e(0, 1)
    loads[2].wait()
    loads[3].wait()
    remote(wg.at[1 - dp], w_send.at[0], w_recv.at[0], twin).wait_recv()
    remote(wu.at[1 - dp], w_send.at[1], w_recv.at[1], twin).wait_recv()
    hidden(0, col)
    step_e(0, 2)
    step_plane(0, 2)
    own_plane(1, 0)
    step_plane(0, 3)
    step_e(0, 3)
    step_z(1, 1)
    hidden(1, y_col)
    hidden(2, x_col)
    step_z(1, 2)
    step_z(1, 3)
    step_diagonal(0)
    hidden(3, d_col)
    for d in range(4):
        step_plane(1, d)
        step_e(1, d)
    for column in (col, y_col, x_col):
        scale(column)
    for k, column in enumerate((col, y_col, x_col, d_col)):
        h_copy(k, column).wait_recv()
    hid_t[...] = jnp.where(flag == 1, hid_other[...].astype(jnp.float32),
                           hid[...].astype(jnp.float32)).T.astype(jnp.bfloat16)
    step_diagonal(1)
    scale(d_col)

    tile = width // TILES

    def product(core, n):
        r = pl.ds(pl.multiple_of(core * mine, mine), mine)
        c = pl.ds(pl.multiple_of(n * tile, tile), tile)
        return jnp.dot(hid_t[r], scaled[:, c], preferred_element_type=jnp.float32).astype(jnp.bfloat16)

    def p_copy(n):
        return remote(part.at[n], p_send.at[n], p_recv.at[n], twin,
                      other_hbm.at[:, pl.ds(n * tile, tile)])

    def o_copy(n):
        return pltpu.make_async_copy(part_own.at[n], sum_hbm.at[:, pl.ds(n * tile, tile)], o_sem.at[n])

    for n in range(TILES):
        part[n] = product(1 - dp, n)
        p_copy(n).start()
    for n in range(TILES):
        part_own[n] = product(dp, n)
        o_copy(n).start()
    for n in range(TILES):
        o_copy(n).wait()
        p_copy(n).wait_recv()

    for a in range(2):
        for s in range(-3, 4):
            @pl.when(valid(s))
            def _(a=a, s=s):
                z_sends(a, s, lambda copy: copy.wait_send())
                z_sends(a, s, lambda copy: copy.wait_send(), e_copy)
                for way in range(2):
                    c_copy(a, way, s, col).wait_send()
                d_copy(a, 0, s, y_col).wait_send()
                d_copy(a, 1, s, x_col).wait_send()
    for copy in weights:
        copy.wait_send()
    for k, column in enumerate((col, y_col, x_col, d_col)):
        h_copy(k, column).wait_send()
    for n in range(TILES):
        p_copy(n).wait_send()


def fused(tokens, cotangent, w_gate, w_up, expert_ids, gate_num, swap_flags):
    rows, width = tokens.shape
    _, half, ff = w_gate.shape
    total, packed = 16 * rows, 16 * SLOTS
    bf16, dma = jnp.bfloat16, pltpu.SemaphoreType.DMA
    hbm = pl.BlockSpec(memory_space=pltpu.HBM)
    term, other = pl.pallas_call(
        kernel,
        out_shape=[jax.ShapeDtypeStruct((ff // 2, width), bf16)] * 2,
        in_specs=[pl.BlockSpec(memory_space=pltpu.SMEM)] + [hbm] * 6,
        out_specs=[hbm, hbm],
        scratch_shapes=[
            pltpu.VMEM((total, width + LANES), bf16),
            pltpu.VMEM((total, width), bf16),
            pltpu.VMEM((2, half, ff), bf16),
            pltpu.VMEM((2, half, ff), bf16),
            pltpu.VMEM((ZS * SLOTS, width), bf16),
            pltpu.VMEM((packed, ff), bf16),
            pltpu.VMEM((packed, ff), bf16),
            pltpu.VMEM((ff, packed), bf16),
            pltpu.VMEM((packed, width), bf16),
            pltpu.VMEM((TILES, ff // 2, width // TILES), bf16),
            pltpu.VMEM((TILES, ff // 2, width // TILES), bf16),
            pltpu.VMEM((expert_ids.shape[1], rows), jnp.int32),
            pltpu.VMEM((expert_ids.shape[1], rows), jnp.int32),
            dma((6,)), dma((2, 2, 3)), dma((2, 2, 3)), dma((2, 2, 7)), dma((2, 2, 7)),
            dma((2, 2, 7)), dma((2, 2, 7)), dma((2, 2, 3)), dma((2, 2, 3)), dma((TILES,)), dma((2,)), dma((2,)), dma((4,)), dma((4,)),
            dma((TILES,)), dma((TILES,)),
        ],
        compiler_params=pltpu.CompilerParams(
            collective_id=0, has_side_effects=True, vmem_limit_bytes=65408 * 1024),
        cost_estimate=pl.CostEstimate(flops=8 * 10**9, bytes_accessed=2 * 10**7, transcendentals=400000),
    )(swap_flags, expert_ids.T, gate_num.T, tokens, cotangent, w_gate[0], w_up[0])
    return (term.astype(jnp.float32) + other.astype(jnp.float32))[None]


def solution(mesh):
    small = mesh.shape["expert"] == 16 and mesh.shape["dp"] == 2
    in_specs = (
        P(("dp", "expert"), None),
        P(("dp", "expert"), None),
        P("expert", "dp", None),
        P("expert", "dp", None),
        P(("dp", "expert"), None),
        P(("dp", "expert"), None),
        P(),
    )
    out_specs = P("expert", "dp", None)
    return jax.shard_map(fused if small else shards, mesh=mesh, in_specs=in_specs, out_specs=out_specs, check_vma=False)
```

```python
import jax
import jax.numpy as jnp
from jax import lax
from jax.experimental import pallas as pl
from jax.experimental.pallas import tpu as pltpu
from jax.sharding import PartitionSpec as P


def from_partner(value, axis, apart):
    return lax.ppermute(value, axis, [(i, i ^ 1 << apart) for i in range(lax.axis_size(axis))])


def shards(tokens, cotangent, w_gate, w_up, expert_ids, gate_num, swap_flags):
    expert_count = lax.axis_size("expert")
    half_count = expert_count // 2
    swap_bit = expert_count.bit_length() - 2
    my_index = lax.axis_index("expert")
    tok_count, top_count = expert_ids.shape
    capacity = 5 * tok_count * top_count // (4 * expert_count)
    width = tokens.shape[1]
    my_flag = swap_flags[my_index % half_count] == 1
    flat_ids = expert_ids.reshape(-1)
    columns = jnp.arange(expert_count, dtype=jnp.int32)
    one_hot = (flat_ids[:, None] == columns[None, :]).astype(jnp.int32)
    ranking = jnp.sum((jnp.cumsum(one_hot, axis=0) - one_hot) * one_hot, axis=1)
    slot_ids = jnp.arange(expert_count * capacity, dtype=jnp.int32)

    def picked_by(destination):
        slot = destination * capacity + ranking
        return (slot_ids[:, None] == slot[None, :]).reshape(
            expert_count * capacity, tok_count, top_count
        )

    token_map = jnp.sum(picked_by(flat_ids).astype(jnp.int32), axis=2).astype(jnp.bfloat16)
    holder = jnp.where(
        swap_flags[flat_ids % half_count] == 1, (flat_ids + half_count) % expert_count, flat_ids
    )
    fractions = gate_num.astype(jnp.float32) / 64.0
    weight_map = jnp.sum(jnp.where(picked_by(holder), fractions[None], 0.0), axis=2).astype(jnp.bfloat16)
    send_rows = jnp.dot(token_map, tokens, preferred_element_type=jnp.float32).astype(jnp.bfloat16)
    send_grads = jnp.dot(weight_map, cotangent, preferred_element_type=jnp.float32).astype(
        jnp.bfloat16
    )

    def exchange(value):
        value = value.reshape(expert_count, capacity, width)
        value = lax.all_to_all(value, "expert", split_axis=0, concat_axis=0, tiled=True)
        return value.reshape(expert_count * capacity, width)

    gate_rows = lax.all_gather(w_gate[0], "dp", axis=0, tiled=True)
    up_rows = lax.all_gather(w_up[0], "dp", axis=0, tiled=True)
    recv_rows = exchange(send_rows)
    gate_sum = jnp.dot(recv_rows, gate_rows, preferred_element_type=jnp.float32)
    up_sum = jnp.dot(recv_rows, up_rows, preferred_element_type=jnp.float32)
    hidden = (jax.nn.silu(gate_sum) * up_sum).astype(jnp.bfloat16)
    other = from_partner(hidden, "expert", swap_bit)
    recv_grads = exchange(send_grads)
    hidden = jnp.where(my_flag, other, hidden)
    grads = lax.psum_scatter(
        lax.dot_general(
            hidden, recv_grads, (((0,), (0,)), ((), ())), preferred_element_type=jnp.float32
        ).astype(jnp.bfloat16),
        "dp",
        scatter_dimension=0,
        tiled=True,
    ).astype(jnp.float32)
    return grads[None]


ZS, LANES, SLOTS, TILES = 4, 128, 32, 5


def kernel(flags_ref, ids_hbm, num_hbm, tok_hbm, cot_hbm, wg_hbm, wu_hbm, sum_hbm, other_hbm,
           tok, cot, wg, wu, picked, hid, hid_other, hid_t, scaled, part, part_own, ids_ref, num_ref,
           local_sem, z_send, z_recv, c_send, c_recv, d_send, d_recv, o_sem,
           w_send, w_recv, h_send, h_recv, p_send, p_recv):
    rows, width = tok_hbm.shape
    count = ids_hbm.shape[0]
    half, ff = wg_hbm.shape
    mine = ff // 2
    experts = 4 * ZS
    dp, me = lax.axis_index("dp"), lax.axis_index("expert")
    x, y, z = me % 2, (me // 2) % 2, me // 4
    to_x, to_y = (dp, me + 1 - 2 * x), (dp, me + 2 - 4 * y)
    up, down = (dp, me + 4), (dp, me - 4)
    pair = (dp, (me + 8) % experts)
    twin = (1 - dp, me)
    col, x_col, y_col = me % 4, me % 4 + 1 - 2 * x, me % 4 + 2 - 4 * y
    d_col = 3 - col

    barrier = pltpu.get_barrier_semaphore()

    def greet(device):
        pl.semaphore_signal(barrier, inc=1, device_id=device, device_id_type=pl.DeviceIdType.MESH)

    for device in (to_x, to_y, pair, twin):
        greet(device)
    pl.when(z < ZS - 1)(lambda: greet(up))
    pl.when(z > 0)(lambda: greet(down))

    def shard(column, s):
        return pl.ds(pl.multiple_of((column * ZS + z + s) * rows, rows), rows)

    def remote(ref, send, recv, device, target=None):
        return pltpu.make_async_remote_copy(
            src_ref=ref, dst_ref=ref if target is None else target, send_sem=send, recv_sem=recv,
            device_id=device, device_id_type=pl.DeviceIdType.MESH)

    own = shard(col, 0)
    loads = [
        pltpu.make_async_copy(tok_hbm, tok.at[own, pl.ds(0, width)], local_sem.at[0]),
        pltpu.make_async_copy(cot_hbm, cot.at[own], local_sem.at[1]),
        pltpu.make_async_copy(wg_hbm, wg.at[dp], local_sem.at[2]),
        pltpu.make_async_copy(wu_hbm, wu.at[dp], local_sem.at[3]),
    ]
    names = [pltpu.make_async_copy(ids_hbm, ids_ref, local_sem.at[4]),
             pltpu.make_async_copy(num_hbm, num_ref, local_sem.at[5])]
    for load in names + loads:
        load.start()
    for load in names:
        load.wait()

    lanes = lax.broadcasted_iota(jnp.int32, (LANES, rows), 0)
    fractions = num_ref[...].astype(jnp.float32) / 64.0
    table = jnp.zeros((LANES, rows), jnp.float32)
    for k in range(count):
        table = jnp.where(lanes == ids_ref[k:k + 1, :], fractions[k:k + 1, :], table)
    same = (lax.broadcasted_iota(jnp.int32, (rows, rows), 0)
            == lax.broadcasted_iota(jnp.int32, (rows, rows), 1))
    tok[own, pl.ds(width, LANES)] = lax.dot_general(
        jnp.where(same, 1.0, 0.0).astype(jnp.bfloat16), table.astype(jnp.bfloat16),
        (((1,), (1,)), ((), ())), preferred_element_type=jnp.float32).astype(jnp.bfloat16)

    inner = (z > 0) & (z < ZS - 1)
    pl.when(inner)(lambda: pl.semaphore_wait(barrier, 6))
    pl.when(jnp.logical_not(inner))(lambda: pl.semaphore_wait(barrier, 5))

    arrays = (tok, cot)

    def valid(s):
        return z + s >= 0 if s < 0 else z + s < ZS

    def z_copy(a, way, d, s):
        return remote(arrays[a].at[shard(col, s)], z_send.at[a, way, d], z_recv.at[a, way, d],
                      up if way == 0 else down)

    def c_copy(a, way, s, column):
        return remote(arrays[a].at[shard(column, s)], c_send.at[a, way, s + 3],
                      c_recv.at[a, way, s + 3], to_x if way == 0 else to_y)

    def d_copy(a, way, s, column):
        size = rows // 2
        start = (column * ZS + z + s) * rows + way * size
        return remote(arrays[a].at[pl.ds(pl.multiple_of(start, size), size)],
                      d_send.at[a, way, s + 3], d_recv.at[a, way, s + 3], to_x if way == 0 else to_y)

    def z_sends(a, s, act):
        if -3 < s <= 0:
            pl.when(z < ZS - 1)(lambda: act(z_copy(a, 0, -s, s)))
        if 0 <= s < 3:
            pl.when(z > 0)(lambda: act(z_copy(a, 1, s, s)))

    def begin(copy):
        copy.start()

    def own_plane(a, s):
        c_copy(a, 0, s, col).start()
        c_copy(a, 1, s, col).start()

    def step_z(a, d):
        for s in (-d, d):
            @pl.when(valid(s))
            def _(s=s):
                z_copy(a, 0 if s < 0 else 1, d - 1, s).wait_recv()
                z_sends(a, s, begin)
                own_plane(a, s)

    def step_plane(a, d):
        for s in ((0,) if d == 0 else (-d, d)):
            @pl.when(valid(s))
            def _(s=s):
                c_copy(a, 1, s, y_col).wait_recv()
                d_copy(a, 0, s, y_col).start()
                c_copy(a, 0, s, x_col).wait_recv()
                d_copy(a, 1, s, x_col).start()

    def step_diagonal(a):
        for s in range(-3, 4):
            @pl.when(valid(s))
            def _(s=s):
                d_copy(a, 0, s, d_col).wait_recv()
                d_copy(a, 1, s, d_col).wait_recv()

    chunk = ZS * rows
    packed = ZS * SLOTS
    flag = flags_ref[me % (experts // 2)]
    held = jnp.where(flag == 1, (me + experts // 2) % experts, me)
    t0 = lax.broadcasted_iota(jnp.int32, (chunk, chunk), 0)
    t1 = lax.broadcasted_iota(jnp.int32, (chunk, chunk), 1)
    earlier = jnp.where((t0 < t1) & (t0 // rows == t1 // rows), 1.0, 0.0).astype(jnp.bfloat16)

    def chosen(column, expert, weighted):
        r = pl.ds(pl.multiple_of(column * chunk, chunk), chunk)
        one = jnp.where(lax.broadcasted_iota(jnp.int32, (16, LANES), 1) == expert, 1.0, 0.0)
        weight = lax.dot_general(one.astype(jnp.bfloat16), tok[r, pl.ds(width, LANES)],
                                 (((1,), (1,)), ((), ())), preferred_element_type=jnp.float32)
        named = jnp.where(weight > 0.0, 1.0, 0.0)
        rank = jnp.dot(named.astype(jnp.bfloat16), earlier, preferred_element_type=jnp.float32)
        place = lax.broadcasted_iota(jnp.int32, (packed, chunk), 0)
        token = lax.broadcasted_iota(jnp.int32, (packed, chunk), 1)
        goal = (place % SLOTS).astype(jnp.float32)
        hit = (goal == rank[0:1]) & (place // SLOTS == token // rows) & (weight[0:1] > 0.0)
        value = weight[0:1] if weighted else named[0:1]
        return jnp.where(hit, value, 0.0).astype(jnp.bfloat16)

    def h_copy(k, column):
        r = pl.ds(pl.multiple_of(column * packed, packed), packed)
        return remote(hid.at[r], h_send.at[k], h_recv.at[k], pair, hid_other.at[r])

    def hidden(k, column):
        r = pl.ds(pl.multiple_of(column * chunk, chunk), chunk)
        h = pl.ds(pl.multiple_of(column * packed, packed), packed)
        take = chosen(column, me, False)

        @pl.loop(0, width // 512)
        def _(n):
            c = pl.ds(pl.multiple_of(n * 512, 512), 512)
            picked[:, c] = jnp.dot(take, tok[r, c], preferred_element_type=jnp.float32).astype(jnp.bfloat16)

        @pl.loop(0, ff // 256)
        def _(n):
            c = pl.ds(pl.multiple_of(n * 256, 256), 256)
            lo, hi = picked[:, 0:half], picked[:, half:2 * half]

            def project(w):
                return (jnp.dot(lo, w[0, :, c], preferred_element_type=jnp.float32)
                        + jnp.dot(hi, w[1, :, c], preferred_element_type=jnp.float32))

            gate, upper = project(wg), project(wu)
            hid[h, c] = (gate / (1.0 + jnp.exp(-gate)) * upper).astype(jnp.bfloat16)

        h_copy(k, column).start()

    def scale(column):
        r = pl.ds(pl.multiple_of(column * chunk, chunk), chunk)
        h = pl.ds(pl.multiple_of(column * packed, packed), packed)
        take = chosen(column, held, True)

        @pl.loop(0, width // 512)
        def _(n):
            c = pl.ds(pl.multiple_of(n * 512, 512), 512)
            scaled[h, c] = jnp.dot(take, cot[r, c], preferred_element_type=jnp.float32).astype(jnp.bfloat16)

    loads[0].wait()
    z_sends(0, 0, begin)
    own_plane(0, 0)
    weights = [remote(wg_hbm, w_send.at[0], w_recv.at[0], twin, wg.at[dp]),
               remote(wu_hbm, w_send.at[1], w_recv.at[1], twin, wu.at[dp])]
    for copy in weights:
        copy.start()
    loads[1].wait()
    step_z(0, 1)
    step_plane(0, 0)
    step_z(0, 2)
    z_sends(1, 0, begin)
    step_plane(0, 1)
    step_z(0, 3)
    loads[2].wait()
    loads[3].wait()
    remote(wg.at[1 - dp], w_send.at[0], w_recv.at[0], twin).wait_recv()
    remote(wu.at[1 - dp], w_send.at[1], w_recv.at[1], twin).wait_recv()
    hidden(0, col)
    step_plane(0, 2)
    step_plane(0, 3)
    own_plane(1, 0)
    step_z(1, 1)
    hidden(1, y_col)
    step_z(1, 2)
    hidden(2, x_col)
    step_z(1, 3)
    step_diagonal(0)
    hidden(3, d_col)
    for d in range(4):
        step_plane(1, d)
    for column in (col, y_col, x_col):
        scale(column)
    for k, column in enumerate((col, y_col, x_col, d_col)):
        h_copy(k, column).wait_recv()
    hid_t[...] = jnp.where(flag == 1, hid_other[...].astype(jnp.float32),
                           hid[...].astype(jnp.float32)).T.astype(jnp.bfloat16)
    step_diagonal(1)
    scale(d_col)

    tile = width // TILES

    def product(core, n):
        r = pl.ds(pl.multiple_of(core * mine, mine), mine)
        c = pl.ds(pl.multiple_of(n * tile, tile), tile)
        return jnp.dot(hid_t[r], scaled[:, c], preferred_element_type=jnp.float32).astype(jnp.bfloat16)

    def p_copy(n):
        return remote(part.at[n], p_send.at[n], p_recv.at[n], twin,
                      other_hbm.at[:, pl.ds(n * tile, tile)])

    def o_copy(n):
        return pltpu.make_async_copy(part_own.at[n], sum_hbm.at[:, pl.ds(n * tile, tile)], o_sem.at[n])

    for n in range(TILES):
        part[n] = product(1 - dp, n)
        p_copy(n).start()
    for n in range(TILES):
        part_own[n] = product(dp, n)
        o_copy(n).start()
    for n in range(TILES):
        o_copy(n).wait()
        p_copy(n).wait_recv()

    for a in range(2):
        for s in range(-3, 4):
            @pl.when(valid(s))
            def _(a=a, s=s):
                z_sends(a, s, lambda copy: copy.wait_send())
                for way in range(2):
                    c_copy(a, way, s, col).wait_send()
                d_copy(a, 0, s, y_col).wait_send()
                d_copy(a, 1, s, x_col).wait_send()
    for copy in weights:
        copy.wait_send()
    for k, column in enumerate((col, y_col, x_col, d_col)):
        h_copy(k, column).wait_send()
    for n in range(TILES):
        p_copy(n).wait_send()


def fused(tokens, cotangent, w_gate, w_up, expert_ids, gate_num, swap_flags):
    rows, width = tokens.shape
    _, half, ff = w_gate.shape
    total, packed = 16 * rows, 16 * SLOTS
    bf16, dma = jnp.bfloat16, pltpu.SemaphoreType.DMA
    hbm = pl.BlockSpec(memory_space=pltpu.HBM)
    term, other = pl.pallas_call(
        kernel,
        out_shape=[jax.ShapeDtypeStruct((ff // 2, width), bf16)] * 2,
        in_specs=[pl.BlockSpec(memory_space=pltpu.SMEM)] + [hbm] * 6,
        out_specs=[hbm, hbm],
        scratch_shapes=[
            pltpu.VMEM((total, width + LANES), bf16),
            pltpu.VMEM((total, width), bf16),
            pltpu.VMEM((2, half, ff), bf16),
            pltpu.VMEM((2, half, ff), bf16),
            pltpu.VMEM((ZS * SLOTS, width), bf16),
            pltpu.VMEM((packed, ff), bf16),
            pltpu.VMEM((packed, ff), bf16),
            pltpu.VMEM((ff, packed), bf16),
            pltpu.VMEM((packed, width), bf16),
            pltpu.VMEM((TILES, ff // 2, width // TILES), bf16),
            pltpu.VMEM((TILES, ff // 2, width // TILES), bf16),
            pltpu.VMEM((expert_ids.shape[1], rows), jnp.int32),
            pltpu.VMEM((expert_ids.shape[1], rows), jnp.int32),
            dma((6,)), dma((2, 2, 3)), dma((2, 2, 3)), dma((2, 2, 7)), dma((2, 2, 7)),
            dma((2, 2, 7)), dma((2, 2, 7)), dma((TILES,)), dma((2,)), dma((2,)), dma((4,)), dma((4,)),
            dma((TILES,)), dma((TILES,)),
        ],
        compiler_params=pltpu.CompilerParams(
            collective_id=0, has_side_effects=True, vmem_limit_bytes=65408 * 1024),
        cost_estimate=pl.CostEstimate(flops=8 * 10**9, bytes_accessed=2 * 10**7, transcendentals=400000),
    )(swap_flags, expert_ids.T, gate_num.T, tokens, cotangent, w_gate[0], w_up[0])
    return (term.astype(jnp.float32) + other.astype(jnp.float32))[None]


def solution(mesh):
    small = mesh.shape["expert"] == 16 and mesh.shape["dp"] == 2
    in_specs = (
        P(("dp", "expert"), None),
        P(("dp", "expert"), None),
        P("expert", "dp", None),
        P("expert", "dp", None),
        P(("dp", "expert"), None),
        P(("dp", "expert"), None),
        P(),
    )
    out_specs = P("expert", "dp", None)
    return jax.shard_map(fused if small else shards, mesh=mesh, in_specs=in_specs, out_specs=out_specs, check_vma=False)
```

```python
import jax
import jax.numpy as jnp
from jax import lax
from jax.experimental import pallas as pl
from jax.experimental.pallas import tpu as pltpu
from jax.sharding import PartitionSpec as P


def from_partner(value, axis, apart):
    return lax.ppermute(value, axis, [(i, i ^ 1 << apart) for i in range(lax.axis_size(axis))])


def shards(tokens, cotangent, w_gate, w_up, expert_ids, gate_num, swap_flags):
    expert_count = lax.axis_size("expert")
    half_count = expert_count // 2
    swap_bit = expert_count.bit_length() - 2
    my_index = lax.axis_index("expert")
    tok_count, top_count = expert_ids.shape
    capacity = 5 * tok_count * top_count // (4 * expert_count)
    width = tokens.shape[1]
    my_flag = swap_flags[my_index % half_count] == 1
    flat_ids = expert_ids.reshape(-1)
    columns = jnp.arange(expert_count, dtype=jnp.int32)
    one_hot = (flat_ids[:, None] == columns[None, :]).astype(jnp.int32)
    ranking = jnp.sum((jnp.cumsum(one_hot, axis=0) - one_hot) * one_hot, axis=1)
    slot_ids = jnp.arange(expert_count * capacity, dtype=jnp.int32)

    def picked_by(destination):
        slot = destination * capacity + ranking
        return (slot_ids[:, None] == slot[None, :]).reshape(
            expert_count * capacity, tok_count, top_count
        )

    token_map = jnp.sum(picked_by(flat_ids).astype(jnp.int32), axis=2).astype(jnp.bfloat16)
    holder = jnp.where(
        swap_flags[flat_ids % half_count] == 1, (flat_ids + half_count) % expert_count, flat_ids
    )
    fractions = gate_num.astype(jnp.float32) / 64.0
    weight_map = jnp.sum(jnp.where(picked_by(holder), fractions[None], 0.0), axis=2).astype(jnp.bfloat16)
    send_rows = jnp.dot(token_map, tokens, preferred_element_type=jnp.float32).astype(jnp.bfloat16)
    send_grads = jnp.dot(weight_map, cotangent, preferred_element_type=jnp.float32).astype(
        jnp.bfloat16
    )

    def exchange(value):
        value = value.reshape(expert_count, capacity, width)
        value = lax.all_to_all(value, "expert", split_axis=0, concat_axis=0, tiled=True)
        return value.reshape(expert_count * capacity, width)

    gate_rows = lax.all_gather(w_gate[0], "dp", axis=0, tiled=True)
    up_rows = lax.all_gather(w_up[0], "dp", axis=0, tiled=True)
    recv_rows = exchange(send_rows)
    gate_sum = jnp.dot(recv_rows, gate_rows, preferred_element_type=jnp.float32)
    up_sum = jnp.dot(recv_rows, up_rows, preferred_element_type=jnp.float32)
    hidden = (jax.nn.silu(gate_sum) * up_sum).astype(jnp.bfloat16)
    other = from_partner(hidden, "expert", swap_bit)
    recv_grads = exchange(send_grads)
    hidden = jnp.where(my_flag, other, hidden)
    grads = lax.psum_scatter(
        lax.dot_general(
            hidden, recv_grads, (((0,), (0,)), ((), ())), preferred_element_type=jnp.float32
        ).astype(jnp.bfloat16),
        "dp",
        scatter_dimension=0,
        tiled=True,
    ).astype(jnp.float32)
    return grads[None]


ZS, LANES, SLOTS, TILES = 4, 128, 32, 5


def kernel(flags_ref, ids_hbm, num_hbm, tok_hbm, cot_hbm, wg_hbm, wu_hbm, sum_hbm, other_hbm,
           tok, cot, wg, wu, picked, hid, hid_other, hid_t, scaled, part, part_own, ids_ref, num_ref,
           local_sem, z_send, z_recv, c_send, c_recv, d_send, d_recv, o_sem,
           w_send, w_recv, h_send, h_recv, p_send, p_recv):
    rows, width = tok_hbm.shape
    count = ids_hbm.shape[0]
    half, ff = wg_hbm.shape
    mine = ff // 2
    experts = 4 * ZS
    dp, me = lax.axis_index("dp"), lax.axis_index("expert")
    x, y, z = me % 2, (me // 2) % 2, me // 4
    to_x, to_y = (dp, me + 1 - 2 * x), (dp, me + 2 - 4 * y)
    up, down = (dp, me + 4), (dp, me - 4)
    pair = (dp, (me + 8) % experts)
    twin = (1 - dp, me)
    col, x_col, y_col = me % 4, me % 4 + 1 - 2 * x, me % 4 + 2 - 4 * y
    d_col = 3 - col

    barrier = pltpu.get_barrier_semaphore()

    def greet(device):
        pl.semaphore_signal(barrier, inc=1, device_id=device, device_id_type=pl.DeviceIdType.MESH)

    for device in (to_x, to_y, pair, twin):
        greet(device)
    pl.when(z < ZS - 1)(lambda: greet(up))
    pl.when(z > 0)(lambda: greet(down))

    def shard(column, s):
        return pl.ds(pl.multiple_of((column * ZS + z + s) * rows, rows), rows)

    def remote(ref, send, recv, device, target=None):
        return pltpu.make_async_remote_copy(
            src_ref=ref, dst_ref=ref if target is None else target, send_sem=send, recv_sem=recv,
            device_id=device, device_id_type=pl.DeviceIdType.MESH)

    own = shard(col, 0)
    loads = [
        pltpu.make_async_copy(tok_hbm, tok.at[own, pl.ds(0, width)], local_sem.at[0]),
        pltpu.make_async_copy(cot_hbm, cot.at[own], local_sem.at[1]),
        pltpu.make_async_copy(wg_hbm, wg.at[dp], local_sem.at[2]),
        pltpu.make_async_copy(wu_hbm, wu.at[dp], local_sem.at[3]),
    ]
    names = [pltpu.make_async_copy(ids_hbm, ids_ref, local_sem.at[4]),
             pltpu.make_async_copy(num_hbm, num_ref, local_sem.at[5])]
    for load in names + loads:
        load.start()
    for load in names:
        load.wait()

    lanes = lax.broadcasted_iota(jnp.int32, (LANES, rows), 0)
    fractions = num_ref[...].astype(jnp.float32) / 64.0
    table = jnp.zeros((LANES, rows), jnp.float32)
    for k in range(count):
        table = jnp.where(lanes == ids_ref[k:k + 1, :], fractions[k:k + 1, :], table)
    same = (lax.broadcasted_iota(jnp.int32, (rows, rows), 0)
            == lax.broadcasted_iota(jnp.int32, (rows, rows), 1))
    tok[own, pl.ds(width, LANES)] = lax.dot_general(
        jnp.where(same, 1.0, 0.0).astype(jnp.bfloat16), table.astype(jnp.bfloat16),
        (((1,), (1,)), ((), ())), preferred_element_type=jnp.float32).astype(jnp.bfloat16)

    inner = (z > 0) & (z < ZS - 1)
    pl.when(inner)(lambda: pl.semaphore_wait(barrier, 6))
    pl.when(jnp.logical_not(inner))(lambda: pl.semaphore_wait(barrier, 5))

    arrays = (tok, cot)

    def valid(s):
        return z + s >= 0 if s < 0 else z + s < ZS

    def z_copy(a, way, d, s):
        return remote(arrays[a].at[shard(col, s)], z_send.at[a, way, d], z_recv.at[a, way, d],
                      up if way == 0 else down)

    def c_copy(a, way, s, column):
        return remote(arrays[a].at[shard(column, s)], c_send.at[a, way, s + 3],
                      c_recv.at[a, way, s + 3], to_x if way == 0 else to_y)

    def d_copy(a, way, s, column):
        size = rows // 2
        start = (column * ZS + z + s) * rows + way * size
        return remote(arrays[a].at[pl.ds(pl.multiple_of(start, size), size)],
                      d_send.at[a, way, s + 3], d_recv.at[a, way, s + 3], to_x if way == 0 else to_y)

    def z_sends(a, s, act):
        if -3 < s <= 0:
            pl.when(z < ZS - 1)(lambda: act(z_copy(a, 0, -s, s)))
        if 0 <= s < 3:
            pl.when(z > 0)(lambda: act(z_copy(a, 1, s, s)))

    def begin(copy):
        copy.start()

    def own_plane(a, s):
        c_copy(a, 0, s, col).start()
        c_copy(a, 1, s, col).start()

    def step_z(a, d):
        for s in (-d, d):
            @pl.when(valid(s))
            def _(s=s):
                z_copy(a, 0 if s < 0 else 1, d - 1, s).wait_recv()
                z_sends(a, s, begin)
                own_plane(a, s)

    def step_plane(a, d):
        for s in ((0,) if d == 0 else (-d, d)):
            @pl.when(valid(s))
            def _(s=s):
                c_copy(a, 1, s, y_col).wait_recv()
                d_copy(a, 0, s, y_col).start()
                c_copy(a, 0, s, x_col).wait_recv()
                d_copy(a, 1, s, x_col).start()

    def step_diagonal(a):
        for s in range(-3, 4):
            @pl.when(valid(s))
            def _(s=s):
                d_copy(a, 0, s, d_col).wait_recv()
                d_copy(a, 1, s, d_col).wait_recv()

    chunk = ZS * rows
    packed = ZS * SLOTS
    flag = flags_ref[me % (experts // 2)]
    held = jnp.where(flag == 1, (me + experts // 2) % experts, me)
    t0 = lax.broadcasted_iota(jnp.int32, (chunk, chunk), 0)
    t1 = lax.broadcasted_iota(jnp.int32, (chunk, chunk), 1)
    earlier = jnp.where((t0 < t1) & (t0 // rows == t1 // rows), 1.0, 0.0).astype(jnp.bfloat16)

    def chosen(column, expert, weighted):
        r = pl.ds(pl.multiple_of(column * chunk, chunk), chunk)
        one = jnp.where(lax.broadcasted_iota(jnp.int32, (16, LANES), 1) == expert, 1.0, 0.0)
        weight = lax.dot_general(one.astype(jnp.bfloat16), tok[r, pl.ds(width, LANES)],
                                 (((1,), (1,)), ((), ())), preferred_element_type=jnp.float32)
        named = jnp.where(weight > 0.0, 1.0, 0.0)
        rank = jnp.dot(named.astype(jnp.bfloat16), earlier, preferred_element_type=jnp.float32)
        place = lax.broadcasted_iota(jnp.int32, (packed, chunk), 0)
        token = lax.broadcasted_iota(jnp.int32, (packed, chunk), 1)
        goal = (place % SLOTS).astype(jnp.float32)
        hit = (goal == rank[0:1]) & (place // SLOTS == token // rows) & (weight[0:1] > 0.0)
        value = weight[0:1] if weighted else named[0:1]
        return jnp.where(hit, value, 0.0).astype(jnp.bfloat16)

    def h_copy(k, column):
        r = pl.ds(pl.multiple_of(column * packed, packed), packed)
        return remote(hid.at[r], h_send.at[k], h_recv.at[k], pair, hid_other.at[r])

    def hidden(k, column):
        r = pl.ds(pl.multiple_of(column * chunk, chunk), chunk)
        h = pl.ds(pl.multiple_of(column * packed, packed), packed)
        take = chosen(column, me, False)

        @pl.loop(0, width // 512)
        def _(n):
            c = pl.ds(pl.multiple_of(n * 512, 512), 512)
            picked[:, c] = jnp.dot(take, tok[r, c], preferred_element_type=jnp.float32).astype(jnp.bfloat16)

        @pl.loop(0, ff // 256)
        def _(n):
            c = pl.ds(pl.multiple_of(n * 256, 256), 256)
            lo, hi = picked[:, 0:half], picked[:, half:2 * half]

            def project(w):
                return (jnp.dot(lo, w[0, :, c], preferred_element_type=jnp.float32)
                        + jnp.dot(hi, w[1, :, c], preferred_element_type=jnp.float32))

            gate, upper = project(wg), project(wu)
            hid[h, c] = (gate / (1.0 + jnp.exp(-gate)) * upper).astype(jnp.bfloat16)

        h_copy(k, column).start()

    def scale(column):
        r = pl.ds(pl.multiple_of(column * chunk, chunk), chunk)
        h = pl.ds(pl.multiple_of(column * packed, packed), packed)
        take = chosen(column, held, True)

        @pl.loop(0, width // 512)
        def _(n):
            c = pl.ds(pl.multiple_of(n * 512, 512), 512)
            scaled[h, c] = jnp.dot(take, cot[r, c], preferred_element_type=jnp.float32).astype(jnp.bfloat16)

    loads[0].wait()
    z_sends(0, 0, begin)
    own_plane(0, 0)
    weights = [remote(wg_hbm, w_send.at[0], w_recv.at[0], twin, wg.at[dp]),
               remote(wu_hbm, w_send.at[1], w_recv.at[1], twin, wu.at[dp])]
    for copy in weights:
        copy.start()
    loads[1].wait()
    step_z(0, 1)
    step_plane(0, 0)
    step_z(0, 2)
    z_sends(1, 0, begin)
    step_plane(0, 1)
    step_z(0, 3)
    loads[2].wait()
    loads[3].wait()
    remote(wg.at[1 - dp], w_send.at[0], w_recv.at[0], twin).wait_recv()
    remote(wu.at[1 - dp], w_send.at[1], w_recv.at[1], twin).wait_recv()
    hidden(0, col)
    step_plane(0, 2)
    own_plane(1, 0)
    step_plane(0, 3)
    step_z(1, 1)
    hidden(1, y_col)
    step_z(1, 2)
    hidden(2, x_col)
    step_z(1, 3)
    step_diagonal(0)
    hidden(3, d_col)
    for d in range(4):
        step_plane(1, d)
    for column in (col, y_col, x_col):
        scale(column)
    for k, column in enumerate((col, y_col, x_col, d_col)):
        h_copy(k, column).wait_recv()
    hid_t[...] = jnp.where(flag == 1, hid_other[...].astype(jnp.float32),
                           hid[...].astype(jnp.float32)).T.astype(jnp.bfloat16)
    step_diagonal(1)
    scale(d_col)

    tile = width // TILES

    def product(core, n):
        r = pl.ds(pl.multiple_of(core * mine, mine), mine)
        c = pl.ds(pl.multiple_of(n * tile, tile), tile)
        return jnp.dot(hid_t[r], scaled[:, c], preferred_element_type=jnp.float32).astype(jnp.bfloat16)

    def p_copy(n):
        return remote(part.at[n], p_send.at[n], p_recv.at[n], twin,
                      other_hbm.at[:, pl.ds(n * tile, tile)])

    def o_copy(n):
        return pltpu.make_async_copy(part_own.at[n], sum_hbm.at[:, pl.ds(n * tile, tile)], o_sem.at[n])

    for n in range(TILES):
        part[n] = product(1 - dp, n)
        p_copy(n).start()
    for n in range(TILES):
        part_own[n] = product(dp, n)
        o_copy(n).start()
    for n in range(TILES):
        o_copy(n).wait()
        p_copy(n).wait_recv()

    for a in range(2):
        for s in range(-3, 4):
            @pl.when(valid(s))
            def _(a=a, s=s):
                z_sends(a, s, lambda copy: copy.wait_send())
                for way in range(2):
                    c_copy(a, way, s, col).wait_send()
                d_copy(a, 0, s, y_col).wait_send()
                d_copy(a, 1, s, x_col).wait_send()
    for copy in weights:
        copy.wait_send()
    for k, column in enumerate((col, y_col, x_col, d_col)):
        h_copy(k, column).wait_send()
    for n in range(TILES):
        p_copy(n).wait_send()


def fused(tokens, cotangent, w_gate, w_up, expert_ids, gate_num, swap_flags):
    rows, width = tokens.shape
    _, half, ff = w_gate.shape
    total, packed = 16 * rows, 16 * SLOTS
    bf16, dma = jnp.bfloat16, pltpu.SemaphoreType.DMA
    hbm = pl.BlockSpec(memory_space=pltpu.HBM)
    term, other = pl.pallas_call(
        kernel,
        out_shape=[jax.ShapeDtypeStruct((ff // 2, width), bf16)] * 2,
        in_specs=[pl.BlockSpec(memory_space=pltpu.SMEM)] + [hbm] * 6,
        out_specs=[hbm, hbm],
        scratch_shapes=[
            pltpu.VMEM((total, width + LANES), bf16),
            pltpu.VMEM((total, width), bf16),
            pltpu.VMEM((2, half, ff), bf16),
            pltpu.VMEM((2, half, ff), bf16),
            pltpu.VMEM((ZS * SLOTS, width), bf16),
            pltpu.VMEM((packed, ff), bf16),
            pltpu.VMEM((packed, ff), bf16),
            pltpu.VMEM((ff, packed), bf16),
            pltpu.VMEM((packed, width), bf16),
            pltpu.VMEM((TILES, ff // 2, width // TILES), bf16),
            pltpu.VMEM((TILES, ff // 2, width // TILES), bf16),
            pltpu.VMEM((expert_ids.shape[1], rows), jnp.int32),
            pltpu.VMEM((expert_ids.shape[1], rows), jnp.int32),
            dma((6,)), dma((2, 2, 3)), dma((2, 2, 3)), dma((2, 2, 7)), dma((2, 2, 7)),
            dma((2, 2, 7)), dma((2, 2, 7)), dma((TILES,)), dma((2,)), dma((2,)), dma((4,)), dma((4,)),
            dma((TILES,)), dma((TILES,)),
        ],
        compiler_params=pltpu.CompilerParams(
            collective_id=0, has_side_effects=True, vmem_limit_bytes=65408 * 1024),
        cost_estimate=pl.CostEstimate(flops=8 * 10**9, bytes_accessed=2 * 10**7, transcendentals=400000),
    )(swap_flags, expert_ids.T, gate_num.T, tokens, cotangent, w_gate[0], w_up[0])
    return (term.astype(jnp.float32) + other.astype(jnp.float32))[None]


def solution(mesh):
    small = mesh.shape["expert"] == 16 and mesh.shape["dp"] == 2
    in_specs = (
        P(("dp", "expert"), None),
        P(("dp", "expert"), None),
        P("expert", "dp", None),
        P("expert", "dp", None),
        P(("dp", "expert"), None),
        P(("dp", "expert"), None),
        P(),
    )
    out_specs = P("expert", "dp", None)
    return jax.shard_map(fused if small else shards, mesh=mesh, in_specs=in_specs, out_specs=out_specs, check_vma=False)
```
